32 devices in a mesh: dp: 16 (over z, y, core), tensor: 2 (over x).
Axes of the slice: x: 2, y: 2, z: 4, core: 2. Of those that a mesh axis runs over, the one named last changes fastest.
Arguments:
- residual: bfloat16 [16384, 768], P(('dp', 'tensor')), may hold values from -6 to 6
- grad_out: bfloat16 [16384, 768], P(('dp', 'tensor')), may hold values from -6 to 6
- norm_gain: float32 [768], replicated, may hold values from 0.5 to 1.5
- w_zx: bfloat16 [2, 768, 1536], P(None, 'dp', 'tensor'), may hold values from -0.21875 to 0.21875
- w_dt: bfloat16 [768, 24], P('dp', 'tensor'), may hold values from -0.21875 to 0.21875
- w_bc: bfloat16 [2, 768, 128], P(None, 'dp'), may hold values from -0.21875 to 0.21875
- conv_x: float32 [4, 1536], P(None, 'tensor'), may hold values from -0.5 to 0.5
- conv_x_bias: float32 [1536], P('tensor'), may hold values from -0.5 to 0.5
- conv_bc: float32 [2, 4, 128], replicated, may hold values from -0.5 to 0.5
- conv_bc_bias: float32 [2, 128], replicated, may hold values from -0.5 to 0.5
- dt_bias: float32 [24], P('tensor'), may hold values from -6 to -2
- a_log: float32 [24], P('tensor'), may hold values from 0 to 2.77
- d_skip: float32 [24], P('tensor'), may hold values from 0.5 to 2
- gate_gain: float32 [1536], P('tensor'), may hold values from 0.5 to 1.5
- w_out: bfloat16 [1536, 768], P('tensor', 'dp'), may hold values from -0.15625 to 0.15625
Outputs:
- layer_out: bfloat16 [16384, 768], P(('dp', 'tensor'))
- d_residual: bfloat16 [16384, 768], P(('dp', 'tensor'))
- g_norm_gain: float32 [768], replicated
- g_w_zx: float32 [2, 768, 1536], P(None, 'dp', 'tensor')
- g_w_dt: float32 [768, 24], P('dp', 'tensor')
- g_w_bc: float32 [2, 768, 128], P(None, 'dp')
- g_conv_x: float32 [4, 1536], P(None, 'tensor')
- g_conv_x_bias: float32 [1536], P('tensor')
- g_conv_bc: float32 [2, 4, 128], replicated
- g_conv_bc_bias: float32 [2, 128], replicated
- g_dt_bias: float32 [24], P('tensor')
- g_a_log: float32 [24], P('tensor')
- g_d_skip: float32 [24], P('tensor')
- g_gate_gain: float32 [1536], P('tensor')
- g_w_out: float32 [1536, 768], P('tensor', 'dp')
The draws below stay inside these ranges and needn't reach their ends.
All inputs are finite; a program needn't handle non-finite values.
Results may differ from the reference program's by a relative error of at most 0.0088.
Values may be sent and summed in bfloat16 or wider, within the bound.
A program may use at most 256 MiB of HBM per device.

```python
import jax
import jax.numpy as jnp
from jax import lax

D = 768
H = 24
P_SIZE = 64
N = 128
K = 4
Q = 256
LEN = 1024
DI = 1536
TOKENS = 16384
N_DP = 16


def block_scale(own_key, shape, shards, least, largest):
    factor_of, own = 1.0, jax.random.fold_in(own_key, 6)
    for position, shards_of in shards:
        steps = jnp.exp(jax.random.uniform(jax.random.fold_in(own, position), (shards_of,), jnp.float32, least / len(shards), largest / len(shards)))
        factor_of = factor_of * jnp.repeat(steps, shape[position] // shards_of).reshape([-1 if axis == position else 1 for axis in range(len(shape))])
    return factor_of


def normal_values(own_key, dims, spread, reach, split=(), kind=jnp.bfloat16):
    gain = block_scale(own_key, dims, split, -0.22, 0.18) if split else 1.0
    result = jax.random.normal(own_key, dims, jnp.float32) * spread * gain
    return jnp.minimum(jnp.maximum(result, -reach), reach).astype(kind)


def setup_inputs(seed: int = 0) -> dict:
    key_list = jax.random.split(jax.random.key(seed), 16)
    residual = normal_values(key_list[0], (TOKENS, D), 1.0, 6.0, ((0, 32),))
    grad_out = normal_values(key_list[1], (TOKENS, D), 1.0, 6.0, ((0, 32),))
    norm_gain = jnp.clip(1.0 + 0.1 * jax.random.normal(key_list[2], (D,), jnp.float32), 0.5, 1.5)
    w_zx = normal_values(key_list[3], (2, D, DI), D ** -0.5, 0.21875, ((1, 16), (2, 2)))
    w_dt = normal_values(key_list[4], (D, H), D ** -0.5, 0.21875, ((0, 16), (1, 2)))
    w_bc = normal_values(key_list[5], (2, D, N), D ** -0.5, 0.21875, ((1, 16),))
    conv_x = jnp.clip(jax.random.uniform(key_list[6], (K, DI), jnp.float32, -0.5, 0.5) * block_scale(key_list[6], (K, DI), ((1, 2),), -0.4, 0.0), -0.5, 0.5)
    conv_x_bias = jnp.clip(jax.random.uniform(key_list[7], (DI,), jnp.float32, -0.5, 0.5) * block_scale(key_list[7], (DI,), ((0, 2),), -0.4, 0.0), -0.5, 0.5)
    conv_bc = jnp.clip(jax.random.uniform(key_list[8], (2, K, N), jnp.float32, -0.5, 0.5), -0.5, 0.5)
    conv_bc_bias = jnp.clip(jax.random.uniform(key_list[9], (2, N), jnp.float32, -0.5, 0.5), -0.5, 0.5)
    dt_bias = jnp.clip(-6.0 + 4.0 * jax.random.uniform(key_list[10], (H,), jnp.float32) ** block_scale(key_list[10], (H,), ((0, 2),), -0.2, 0.2), -6.0, -2.0)
    a_log = jnp.clip(2.77 * jax.random.uniform(key_list[11], (H,), jnp.float32) ** block_scale(key_list[11], (H,), ((0, 2),), -0.2, 0.2), 0.0, 2.77)
    d_skip = jnp.clip(0.5 + 1.5 * jax.random.uniform(key_list[12], (H,), jnp.float32) ** block_scale(key_list[12], (H,), ((0, 2),), -0.2, 0.2), 0.5, 2.0)
    gate_gain = jnp.clip(1.0 + 0.1 * jax.random.normal(key_list[13], (DI,), jnp.float32), 0.5, 1.5)
    w_out = normal_values(key_list[14], (DI, D), DI ** -0.5, 0.15625, ((0, 2), (1, 16)))
    return {"residual": residual, "grad_out": grad_out, "norm_gain": norm_gain, "w_zx": w_zx, "w_dt": w_dt, "w_bc": w_bc, "conv_x": conv_x, "conv_x_bias": conv_x_bias, "conv_bc": conv_bc, "conv_bc_bias": conv_bc_bias, "dt_bias": dt_bias, "a_log": a_log, "d_skip": d_skip, "gate_gain": gate_gain, "w_out": w_out}


@jax.custom_vjp
def low(v):
    return lax.optimization_barrier(v.astype(jnp.bfloat16)).astype(jnp.float32)

@jax.custom_vjp
def low_back(v):
    return v

def low_keep(v):
    return (low(v), None)

def low_pass(kept, grad):
    return (grad,)

def back_keep(v):
    return (v, None)

def back_low(kept, grad):
    return (low(grad),)
low.defvjp(low_keep, low_pass)
low_back.defvjp(back_keep, back_low)
EPS = 1e-05
HIGH = lax.Precision.HIGHEST

def causal_conv(sequence, kernel, conv_bias):
    taps = kernel.shape[0]
    padded = jnp.pad(sequence, ((taps - 1, 0), (0, 0)))
    summed = jnp.zeros_like(sequence) + conv_bias[None, :]
    for offset in range(taps):
        summed = summed + kernel[offset][None, :] * padded[offset:offset + sequence.shape[0]]
    return summed

def ssd_block(memory, pieces):
    signal, inject, readout, timestep, decays = pieces
    running = jnp.cumsum(decays, axis=0)
    row_index = jnp.arange(signal.shape[0])
    causal_mask = (row_index[:, None] >= row_index[None, :])[:, :, None]
    weights = jnp.exp(jnp.where(causal_mask, running[:, None, :] - running[None, :, :], -jnp.inf))
    affinity = jnp.dot(readout, inject.T, precision=HIGH)
    mixing = affinity[:, :, None] * weights * timestep[None, :, :]
    within = jnp.einsum('ijh,jhp->ihp', mixing, signal, precision=HIGH)
    across = jnp.exp(running)[:, :, None] * jnp.einsum('hpn,in->ihp', memory, readout, precision=HIGH)
    to_end = jnp.exp(running[-1][None, :] - running) * timestep
    carried = jnp.exp(running[-1])[:, None, None] * memory + jnp.einsum('jh,jhp,jn->hpn', to_end, signal, inject, precision=HIGH)
    return (carried, within + across)

def ssd_sequence(signal, inject, readout, timestep, decays):
    length = signal.shape[0]

    def by_block(array):
        return array.reshape((length // Q, Q) + array.shape[1:])
    initial = jnp.zeros((H, P_SIZE, N), jnp.float32)
    _, outputs = lax.scan(jax.checkpoint(ssd_block), initial, (by_block(signal), by_block(inject), by_block(readout), by_block(timestep), by_block(decays)))
    return outputs.reshape(signal.shape)

def layer(residual, norm_gain, w_zx, w_dt, w_bc, conv_x, conv_x_bias, conv_bc, conv_bc_bias, dt_bias, a_log, d_skip, gate_gain, w_out):
    in_scale = lax.rsqrt(lax.optimization_barrier(jnp.mean(residual * residual, axis=1, keepdims=True)) + EPS)
    normed = low(residual * in_scale * norm_gain)
    gate_pre = low_back(jnp.dot(normed, w_zx[0], precision=HIGH))
    x_pre = low_back(jnp.dot(normed, w_zx[1], precision=HIGH))
    dt_raw = low_back(jnp.dot(normed, w_dt, precision=HIGH))
    b_raw = low_back(jnp.dot(normed, w_bc[0], precision=HIGH))
    c_raw = low_back(jnp.dot(normed, w_bc[1], precision=HIGH))
    signal = low(jax.nn.silu(causal_conv(x_pre, conv_x, conv_x_bias)))
    inject = low(jax.nn.silu(causal_conv(b_raw, conv_bc[0], conv_bc_bias[0])))
    readout = low(jax.nn.silu(causal_conv(c_raw, conv_bc[1], conv_bc_bias[1])))
    timestep = jax.nn.softplus(dt_raw + dt_bias)
    decays = -timestep * jnp.exp(a_log)
    scanned = ssd_sequence(signal.reshape(LEN, H, P_SIZE), inject, readout, timestep, decays)
    mixed = scanned.reshape(LEN, H * P_SIZE) + jnp.repeat(d_skip, P_SIZE) * signal
    gated_in = mixed * jax.nn.silu(gate_pre)
    out_scale = lax.rsqrt(lax.optimization_barrier(jnp.mean(gated_in * gated_in, axis=1, keepdims=True)) + EPS)
    gated = low(gated_in * out_scale * gate_gain)
    return residual + jnp.dot(gated, w_out, precision=HIGH)

def reference(residual, grad_out, norm_gain, w_zx, w_dt, w_bc, conv_x, conv_x_bias, conv_bc, conv_bc_bias, dt_bias, a_log, d_skip, gate_gain, w_out):
    params = tuple((array.astype(jnp.float32) for array in (norm_gain, w_zx, w_dt, w_bc, conv_x, conv_x_bias, conv_bc, conv_bc_bias, dt_bias, a_log, d_skip, gate_gain, w_out)))

    def forward(whole, *weights):
        sequences = whole.reshape(N_DP, LEN, D)
        results = lax.map(lambda single: jax.checkpoint(layer)(single, *weights), sequences)
        return results.reshape(TOKENS, D)
    layer_out, backward = jax.vjp(forward, residual.astype(jnp.float32), *params)
    grads = backward(grad_out.astype(jnp.float32))
    return (layer_out.astype(jnp.bfloat16), grads[0].astype(jnp.bfloat16), grads[1], grads[2], grads[3], grads[4], grads[5], grads[6], grads[7], grads[8], grads[9], grads[10], grads[11], grads[12], grads[13])
```

```python
import functools

import jax
import jax.numpy as jnp
from jax import lax
from jax.experimental import pallas as pl
from jax.experimental.pallas import tpu as pltpu
from jax.sharding import PartitionSpec as P

Q = 256
EPS = 1e-05
HIGH = lax.Precision.HIGHEST
F32 = jnp.float32
BF16 = jnp.bfloat16
NN = (((1,), (0,)), ((), ()))
NT = (((1,), (1,)), ((), ()))
TN = (((0,), (0,)), ((), ()))
LANES = 128
DT_AT = 16


def dot(a, b, dims=NN):
    return lax.dot_general(a, b, dims, preferred_element_type=F32)


def rows_of(ref, first, count, columns):
    return ref[pl.ds(first, count), columns]


def scan_forward(heads, taps, xp_ref, col_ref, row_ref, w_ref, skip_ref, mixed_ref, pre_ref, states_ref, buf, act, st):
    channels = skip_ref.shape[1]
    wide = xp_ref.shape[1]
    state_size = (wide - channels) // 2

    @pl.when(pl.program_id(0) == 0)
    def _():
        st[...] = jnp.zeros_like(st)
        buf[0:8, :] = jnp.zeros((8, wide), F32)

    buf[8 : 8 + Q, :] = xp_ref[...]
    for start in range(0, wide, LANES):
        cols = pl.ds(start, LANES)
        pre = w_ref[taps : taps + 1, cols] + jnp.zeros((Q, LANES), F32)
        for k in range(taps):
            pre = pre + w_ref[k : k + 1, cols] * buf[9 - taps + k : 9 - taps + k + Q, cols]
        pre_ref[:, cols] = pre
        act[:, cols] = (pre * jax.nn.sigmoid(pre)).astype(BF16)
    buf[0:8, :] = buf[Q : Q + 8, :]

    inject = act[:, channels : channels + state_size]
    readout = act[:, channels + state_size :]
    affinity = dot(readout, inject, NT)
    mask = lax.broadcasted_iota(jnp.int32, (Q, Q), 0) >= lax.broadcasted_iota(jnp.int32, (Q, Q), 1)
    first = lax.broadcasted_iota(jnp.int32, (1, LANES), 1) < LANES // 2
    states_ref[0] = st[...].astype(BF16)
    for pair in range(heads // 2):
        cols = pl.ds(pair * LANES, LANES)
        signal = act[:, cols]
        parts = []
        for side in range(2):
            h = 2 * pair + side
            gap = col_ref[:, h : h + 1] - row_ref[h : h + 1, :]
            weights = jnp.where(mask, jnp.exp(gap), 0.0)
            mixing = (affinity * weights * row_ref[DT_AT + h : DT_AT + h + 1, :]).astype(BF16)
            parts.append(dot(mixing, signal))
        within = jnp.where(first, parts[0], parts[1])
        run = jnp.where(first, col_ref[:, 2 * pair : 2 * pair + 1], col_ref[:, 2 * pair + 1 : 2 * pair + 2])
        step = jnp.where(
            first,
            col_ref[:, DT_AT + 2 * pair : DT_AT + 2 * pair + 1],
            col_ref[:, DT_AT + 2 * pair + 1 : DT_AT + 2 * pair + 2],
        )
        end = run[Q - 1 : Q, :]
        before = st[:, cols]
        across = jnp.exp(run) * dot(readout, before.astype(BF16))
        wide_signal = signal.astype(F32)
        mixed_ref[:, cols] = within + across + skip_ref[:, cols] * wide_signal
        weighted = (jnp.exp(end - run) * step * wide_signal).astype(BF16)
        st[:, cols] = jnp.exp(end) * before + dot(inject, weighted, TN)


def scan_backward(
    heads, taps, xp_ref, pre_ref, col_ref, row_ref, w_ref, skip_ref, states_ref, dy_ref,
    dx_ref, dbc_ref, colout_ref, rowout_ref, sums_ref, gw_ref, buf, dst, dgs,
):
    channels = skip_ref.shape[1]
    wide = xp_ref.shape[1]
    state_size = (wide - channels) // 2

    @pl.when(pl.program_id(0) == 0)
    def _():
        dst[...] = jnp.zeros_like(dst)
        buf[Q : Q + 8, :] = jnp.zeros((8, wide), F32)
        gw_ref[...] = jnp.zeros_like(gw_ref)

    def act_of(start):
        pre = pre_ref[:, pl.ds(start, LANES)]
        return (pre * jax.nn.sigmoid(pre)).astype(BF16)

    def conv_back(start, d_act):
        cols = pl.ds(start, LANES)
        pre = pre_ref[:, cols]
        s = jax.nn.sigmoid(pre)
        d_pre = d_act * s * (1.0 + pre * (1.0 - s))
        buf[0:Q, cols] = d_pre
        own = xp_ref[:, cols]
        total = jnp.zeros((Q, LANES), F32)
        for k in range(taps):
            moved = buf[taps - 1 - k : taps - 1 - k + Q, cols]
            total = total + w_ref[k : k + 1, cols] * moved
            gw_ref[k : k + 1, cols] += jnp.sum(own * moved, axis=0, keepdims=True)
        gw_ref[taps : taps + 1, cols] += jnp.sum(d_pre, axis=0, keepdims=True)
        buf[Q : Q + 8, cols] = d_pre[0:8, :]
        return total.astype(BF16)

    inject = act_of(channels)
    readout = act_of(channels + state_size)
    affinity = dot(readout, inject, NT)
    mask = lax.broadcasted_iota(jnp.int32, (Q, Q), 0) >= lax.broadcasted_iota(jnp.int32, (Q, Q), 1)
    lane = lax.broadcasted_iota(jnp.int32, (1, LANES), 1)
    first = lane < LANES // 2
    d_inject = jnp.zeros((Q, state_size), F32)
    d_readout = jnp.zeros((Q, state_size), F32)
    colout = jnp.zeros((Q, LANES), F32)
    dgs[...] = jnp.zeros_like(dgs)
    for pair in range(heads // 2):
        cols = pl.ds(pair * LANES, LANES)
        signal = act_of(pair * LANES)
        wide_signal = signal.astype(F32)
        d_low = dy_ref[:, cols]
        d_wide = d_low.astype(F32)
        before = states_ref[0, :, cols]
        d_after = dst[:, cols]
        d_after_low = d_after.astype(BF16)
        run = jnp.where(first, col_ref[:, 2 * pair : 2 * pair + 1], col_ref[:, 2 * pair + 1 : 2 * pair + 2])
        step = jnp.where(
            first,
            col_ref[:, DT_AT + 2 * pair : DT_AT + 2 * pair + 1],
            col_ref[:, DT_AT + 2 * pair + 1 : DT_AT + 2 * pair + 2],
        )
        end = run[Q - 1 : Q, :]
        grown = jnp.exp(run)
        to_end = jnp.exp(end - run)
        d_across = (grown * d_wide).astype(BF16)
        across_part = grown * d_wide * dot(readout, before)
        from_state = dot(inject, d_after_low)
        end_part = wide_signal * from_state
        d_readout += dot(d_across, before, NT)
        d_inject += dot((to_end * step * wide_signal).astype(BF16), d_after_low, NT)
        parts = []
        for side in range(2):
            h = 2 * pair + side
            mine = first if side == 0 else ~first
            gap = col_ref[:, h : h + 1] - row_ref[h : h + 1, :]
            weights = jnp.where(mask, jnp.exp(gap), 0.0)
            stepped = weights * row_ref[DT_AT + h : DT_AT + h + 1, :]
            plain = affinity * weights
            d_mixing = dot(d_low, jnp.where(mine, signal, jnp.zeros_like(signal)), NT)
            dgs[...] += d_mixing * stepped
            pulled = d_mixing * plain
            rowout_ref[h : h + 1, :] = jnp.sum(pulled, axis=0, keepdims=True)
            along = jnp.sum(pulled * row_ref[DT_AT + h : DT_AT + h + 1, :], axis=1, keepdims=True)
            along = along + jnp.sum(jnp.where(mine, across_part, 0.0), axis=1, keepdims=True)
            ended = jnp.sum(jnp.where(mine, end_part, 0.0), axis=1, keepdims=True)
            colout = jnp.where(lane == h, along, colout)
            colout = jnp.where(lane == DT_AT + h, ended, colout)
            parts.append(dot(plain.astype(BF16), d_low, TN))
        within = jnp.where(first, parts[0], parts[1])
        d_signal = step * (within + to_end * from_state) + skip_ref[:, cols] * d_wide
        grown_end = jnp.exp(end)
        sums_ref[0, 0:1, cols] = grown_end * jnp.sum(d_after * before.astype(F32), axis=0, keepdims=True)
        sums_ref[0, 1:2, cols] = jnp.sum(d_wide * wide_signal, axis=0, keepdims=True)
        dst[:, cols] = grown_end * d_after + dot(readout, d_across, TN)
        dx_ref[:, cols] = conv_back(pair * LANES, d_signal)
    colout_ref[...] = colout
    d_affinity = dgs[...].astype(BF16)
    d_readout += dot(d_affinity, inject)
    d_inject += dot(d_affinity, readout, TN)
    dbc_ref[:, :state_size] = conv_back(channels, d_inject)
    dbc_ref[:, state_size:] = conv_back(channels + state_size, d_readout)


def whole_block(shape):
    return pl.BlockSpec(shape, lambda i: (0,) * len(shape))


def run_forward(xp, col, row, w, skip, heads, taps):
    length, wide = xp.shape[0], w.shape[1]
    channels = skip.shape[1]
    chunks = length // Q
    state_size = (wide - channels) // 2
    return pl.pallas_call(
        functools.partial(scan_forward, heads, taps),
        grid=(chunks,),
        in_specs=[
            pl.BlockSpec((Q, wide), lambda i: (i, 0)),
            pl.BlockSpec((Q, LANES), lambda i: (i, 0)),
            pl.BlockSpec((2 * DT_AT, Q), lambda i: (0, i)),
            whole_block(w.shape),
            whole_block(skip.shape),
        ],
        out_specs=[
            pl.BlockSpec((Q, channels), lambda i: (i, 0)),
            pl.BlockSpec((Q, wide), lambda i: (i, 0)),
            pl.BlockSpec((1, state_size, channels), lambda i: (i, 0, 0)),
        ],
        out_shape=[
            jax.ShapeDtypeStruct((length, channels), F32),
            jax.ShapeDtypeStruct((length, wide), F32),
            jax.ShapeDtypeStruct((chunks, state_size, channels), BF16),
        ],
        scratch_shapes=[
            pltpu.VMEM((Q + 8, wide), F32),
            pltpu.VMEM((Q, wide), BF16),
            pltpu.VMEM((state_size, channels), F32),
        ],
        compiler_params=pltpu.CompilerParams(vmem_limit_bytes=40 * 2**20),
        cost_estimate=pl.CostEstimate(flops=20 * 10**9, bytes_accessed=13 * 10**6, transcendentals=5 * 10**6),
        name="scan_forward",
    )(xp, col, row, w, skip)


def run_backward(xp, pre, col, row, w, skip, states, dy, heads, taps):
    length, wide = pre.shape
    channels = skip.shape[1]
    chunks = length // Q
    state_size = (wide - channels) // 2
    back = lambda i: (chunks - 1 - i, 0)
    return pl.pallas_call(
        functools.partial(scan_backward, heads, taps),
        grid=(chunks,),
        in_specs=[
            pl.BlockSpec((Q, wide), back),
            pl.BlockSpec((Q, wide), back),
            pl.BlockSpec((Q, LANES), back),
            pl.BlockSpec((2 * DT_AT, Q), lambda i: (0, chunks - 1 - i)),
            whole_block(w.shape),
            whole_block(skip.shape),
            pl.BlockSpec((1, state_size, channels), lambda i: (chunks - 1 - i, 0, 0)),
            pl.BlockSpec((Q, channels), back),
        ],
        out_specs=[
            pl.BlockSpec((Q, channels), back),
            pl.BlockSpec((Q, 2 * state_size), back),
            pl.BlockSpec((Q, LANES), back),
            pl.BlockSpec((DT_AT, Q), lambda i: (0, chunks - 1 - i)),
            pl.BlockSpec((1, 2, channels), lambda i: (chunks - 1 - i, 0, 0)),
            whole_block(w.shape),
        ],
        out_shape=[
            jax.ShapeDtypeStruct((length, channels), BF16),
            jax.ShapeDtypeStruct((length, 2 * state_size), BF16),
            jax.ShapeDtypeStruct((length, LANES), F32),
            jax.ShapeDtypeStruct((DT_AT, length), F32),
            jax.ShapeDtypeStruct((chunks, 2, channels), F32),
            jax.ShapeDtypeStruct(w.shape, F32),
        ],
        scratch_shapes=[
            pltpu.VMEM((Q + 8, wide), F32),
            pltpu.VMEM((state_size, channels), F32),
            pltpu.VMEM((Q, Q), F32),
        ],
        compiler_params=pltpu.CompilerParams(vmem_limit_bytes=40 * 2**20),
        cost_estimate=pl.CostEstimate(flops=40 * 10**9, bytes_accessed=15 * 10**6, transcendentals=5 * 10**6),
        name="scan_backward",
    )(xp, pre, col, row, w, skip, states, dy)


def swap(x, axis, bit):
    size = lax.axis_size(axis)
    return lax.ppermute(x, axis, [(i, i ^ bit) for i in range(size)])


def bits_of(axis):
    size = lax.axis_size(axis)
    return [1 << k for k in range(size.bit_length() - 1)]


def my_bit(axis, bit):
    return (lax.axis_index(axis) // bit) % 2


def both(own, other, second):
    return jnp.where(second == 1, jnp.stack([other, own]), jnp.stack([own, other]))


def gather_rows(block):
    bits = bits_of("dp")
    order = [b for b in bits if b > 2] + [b for b in bits if b == 2] + [b for b in bits if b == 1]
    x = block
    for bit in order:
        x = both(x, swap(x, "dp", bit), my_bit("dp", bit))
    done = order[::-1]
    axes = [done.index(b) for b in bits[::-1]]
    count = len(bits)
    x = jnp.transpose(x, axes + list(range(count, count + block.ndim)))
    return x.reshape((-1,) + block.shape[1:])


def scatter_rows(x):
    bits = bits_of("dp")
    left = bits[::-1]
    x = x.reshape((2,) * len(bits) + (x.shape[0] >> len(bits), x.shape[1]))
    for bit in bits:
        axis = left.index(bit)
        mine = my_bit("dp", bit)
        keep = lax.dynamic_index_in_dim(x, mine, axis, keepdims=False)
        send = lax.dynamic_index_in_dim(x, 1 - mine, axis, keepdims=False).astype(BF16)
        x = keep.astype(F32) + swap(send, "dp", bit).astype(F32)
        left.remove(bit)
    return x


def sum_dp(x):
    for bit in bits_of("dp"):
        x = x + swap(x, "dp", bit)
    return x


def body(
    residual, grad_out, norm_gain, w_zx, w_dt, w_bc, conv_x, conv_x_bias, conv_bc, conv_bc_bias,
    dt_bias, a_log, d_skip, gate_gain, w_out,
):
    own_rows, width = residual.shape
    channels = gate_gain.shape[0]
    all_channels = channels * lax.axis_size("tensor")
    state_size = w_bc.shape[2]
    heads = dt_bias.shape[0]
    head_size = channels // heads
    taps = conv_x.shape[0]
    wide = channels + 2 * state_size
    side = lax.axis_index("tensor")

    def own_half(x):
        return lax.dynamic_slice_in_dim(x, side * own_rows, own_rows, 0)

    def other_half(x):
        return lax.dynamic_slice_in_dim(x, (1 - side) * own_rows, own_rows, 0)

    pad_dt = LANES - heads
    weights_in = gather_rows(
        jnp.concatenate([w_zx[1], w_bc[0], w_bc[1], jnp.pad(w_dt, ((0, 0), (0, pad_dt)))], axis=1)
    )
    weights_side = gather_rows(jnp.concatenate([w_zx[0], w_out.T], axis=1))
    weight_gate, weight_out_t = weights_side[:, :channels], weights_side[:, channels:]

    rows = both(residual, swap(residual, "tensor", 1), side).reshape(2 * own_rows, width).astype(F32)
    cotangent = both(grad_out, swap(grad_out, "tensor", 1), side).reshape(2 * own_rows, width)
    in_scale = lax.rsqrt(jnp.mean(rows * rows, axis=1, keepdims=True) + EPS)
    normed = (rows * in_scale * norm_gain).astype(BF16)

    projected = dot(normed, weights_in)
    dt_in = projected[:, wide : wide + heads] + dt_bias
    timestep = jax.nn.softplus(dt_in)
    rate = -jnp.exp(a_log)
    decays = timestep * rate
    length = decays.shape[0]
    chunks = length // Q
    tri = jnp.tril(jnp.ones((Q, Q), F32))
    running = jnp.einsum("ij,cjh->cih", tri, decays.reshape(chunks, Q, heads), precision=HIGH)
    running_flat = running.reshape(length, heads)
    gap = jnp.zeros((length, DT_AT - heads), F32)
    packed = jnp.concatenate([running_flat, gap, timestep, gap], axis=1)
    col = jnp.pad(packed, ((0, 0), (0, LANES - 2 * DT_AT)))
    row = packed.T
    taps_all = jnp.concatenate([conv_x, conv_bc[0], conv_bc[1]], axis=1)
    bias_all = jnp.concatenate([conv_x_bias, conv_bc_bias[0], conv_bc_bias[1]])
    w = jnp.concatenate([taps_all, bias_all[None], jnp.zeros((8 - taps - 1, wide), F32)], axis=0)
    skip = jnp.repeat(d_skip, head_size)[None]
    mixed, pre, states = run_forward(projected, col, row, w, skip, heads, taps)

    gate_pre = dot(normed, weight_gate)
    d_gated = dot(cotangent, weight_out_t)
    logistic = jax.nn.sigmoid(gate_pre)
    gate_act = gate_pre * logistic
    gated_in = mixed * gate_act
    scaled_grad = d_gated * gate_gain
    sums = jnp.stack([jnp.sum(gated_in * gated_in, axis=1), jnp.sum(scaled_grad * gated_in, axis=1)])
    sums = sums + swap(sums, "tensor", 1)
    out_scale = lax.rsqrt(sums[0] / all_channels + EPS)[:, None]
    gated = (gated_in * out_scale * gate_gain).astype(BF16)
    d_inner = out_scale * scaled_grad - gated_in * (out_scale**3 * sums[1][:, None] / all_channels)
    d_mixed = (d_inner * gate_act).astype(BF16)
    d_gate = (d_inner * mixed * logistic * (1.0 + gate_pre * (1.0 - logistic))).astype(BF16)
    grad_gate_gain = jnp.sum(d_gated * gated_in * out_scale, axis=0)

    sent = swap(dot(other_half(gated), weight_out_t, NT).astype(BF16), "tensor", 1)
    branch = dot(own_half(gated), weight_out_t, NT) + sent.astype(F32)
    layer_out = (residual.astype(F32) + branch).astype(BF16)

    grad_side = scatter_rows(
        jnp.concatenate([dot(normed, d_gate, TN), dot(cotangent, gated, TN)], axis=1)
    )
    d_x, d_bc, colout, rowout, chunk_sums, grad_w = run_backward(
        projected, pre, col, row, w, skip, states, d_mixed, heads, taps
    )

    along = colout[:, :heads].reshape(chunks, Q, heads)
    ended = colout[:, DT_AT : DT_AT + heads].reshape(chunks, Q, heads)
    pulled = rowout[:heads].T.reshape(chunks, Q, heads)
    steps = timestep.reshape(chunks, Q, heads)
    d_step = pulled + jnp.exp(running[:, -1:] - running) * ended
    to_end = steps * jnp.exp(running[:, -1:] - running) * ended
    d_running = along - steps * d_step
    per_head = jnp.sum(chunk_sums.reshape(chunks, 2, heads, head_size), axis=3)
    at_end = jnp.sum(to_end, axis=1) + per_head[:, 0]
    d_decays = jnp.einsum("ji,cjh->cih", tri, d_running, precision=HIGH) + at_end[:, None]
    d_decays = d_decays.reshape(length, heads)
    d_dt = (d_step.reshape(length, heads) + d_decays * rate) * jax.nn.sigmoid(dt_in)
    grad_dt_bias = jnp.sum(d_dt, axis=0)
    grad_a_log = jnp.sum(d_decays * decays, axis=0)
    grad_d_skip = jnp.sum(per_head[:, 1], axis=0)

    d_shared = d_bc.astype(F32) + swap(d_bc, "tensor", 1).astype(F32)
    d_shared = d_shared.astype(BF16)
    d_dt_low = jnp.pad(d_dt.astype(BF16), ((0, 0), (0, pad_dt)))
    grad_in = scatter_rows(dot(normed, jnp.concatenate([d_x, d_shared, d_dt_low], axis=1), TN))
    d_all = jnp.concatenate([d_x, d_shared * 0.5, d_dt_low, d_gate], axis=1)
    weights_all = jnp.concatenate([weights_in, weight_gate], axis=1)
    partial = dot(d_all, weights_all, NT)
    received = swap(other_half(partial).astype(BF16), "tensor", 1)
    grad_norm_gain = jnp.sum(partial * rows * in_scale, axis=0)

    shared = jnp.concatenate([grad_norm_gain, grad_w[: taps + 1, channels:].reshape(-1)])
    shared = shared + swap(shared, "tensor", 1)
    heads_part = jnp.concatenate([grad_dt_bias, grad_a_log, grad_d_skip])
    small = jnp.concatenate(
        [grad_gate_gain, grad_w[: taps + 1, :channels].reshape(-1), shared, heads_part]
    )
    count = small.shape[0]
    small = jnp.pad(small, (0, -count % 1024)).reshape(-1, LANES)
    small = sum_dp(small).reshape(-1)
    pieces, at = [], 0
    for size in (channels, (taps + 1) * channels, width, (taps + 1) * 2 * state_size, heads, heads, heads):
        pieces.append(small[at : at + size])
        at += size
    sum_gate_gain, sum_conv, sum_norm, sum_bc, sum_dt_bias, sum_a_log, sum_skip = pieces
    sum_conv = sum_conv.reshape(taps + 1, channels)
    sum_bc = sum_bc.reshape(taps + 1, 2, state_size).transpose(1, 0, 2)

    d_normed = own_half(partial) + received.astype(F32)
    own_scale = own_half(in_scale)
    own = residual.astype(F32)
    weighted = d_normed * norm_gain
    d_residual = (
        grad_out.astype(F32)
        + own_scale * weighted
        - own * own_scale**3 * jnp.mean(weighted * own, axis=1, keepdims=True)
    ).astype(BF16)
    return (
        layer_out,
        d_residual,
        sum_norm,
        jnp.stack([grad_side[:, :channels], grad_in[:, :channels]]),
        grad_in[:, wide : wide + heads],
        jnp.stack([grad_in[:, channels : channels + state_size], grad_in[:, channels + state_size : wide]]),
        sum_conv[:taps],
        sum_conv[taps],
        sum_bc[:, :taps],
        sum_bc[:, taps],
        sum_dt_bias,
        sum_a_log,
        sum_skip,
        sum_gate_gain,
        grad_side[:, channels:].T,
    )


def solution(mesh):
    in_specs = (
        P(("dp", "tensor"), None),
        P(("dp", "tensor"), None),
        P(),
        P(None, "dp", "tensor"),
        P("dp", "tensor"),
        P(None, "dp", None),
        P(None, "tensor"),
        P("tensor"),
        P(),
        P(),
        P("tensor"),
        P("tensor"),
        P("tensor"),
        P("tensor"),
        P("tensor", "dp"),
    )
    out_specs = (
        P(("dp", "tensor"), None),
        P(("dp", "tensor"), None),
        P(),
        P(None, "dp", "tensor"),
        P("dp", "tensor"),
        P(None, "dp", None),
        P(None, "tensor"),
        P("tensor"),
        P(),
        P(),
        P("tensor"),
        P("tensor"),
        P("tensor"),
        P("tensor"),
        P("tensor", "dp"),
    )
    return jax.shard_map(body, mesh=mesh, in_specs=in_specs, out_specs=out_specs, check_vma=False)
```

```python
import functools

import jax
import jax.numpy as jnp
from jax import lax
from jax.experimental import pallas as pl
from jax.experimental.pallas import tpu as pltpu
from jax.sharding import PartitionSpec as P

Q = 256
EPS = 1e-05
HIGH = lax.Precision.HIGHEST
F32 = jnp.float32
BF16 = jnp.bfloat16
NN = (((1,), (0,)), ((), ()))
NT = (((1,), (1,)), ((), ()))
TN = (((0,), (0,)), ((), ()))
LANES = 128
DT_AT = 16


def dot(a, b, dims=NN):
    return lax.dot_general(a, b, dims, preferred_element_type=F32)


def rows_of(ref, first, count, columns):
    return ref[pl.ds(first, count), columns]


def scan_forward(heads, taps, xp_ref, col_ref, row_ref, w_ref, skip_ref, _, mixed_ref, pre_ref, states_ref, buf, act, st):
    channels = skip_ref.shape[1]
    wide = xp_ref.shape[1]
    state_size = (wide - channels) // 2

    @pl.when(pl.program_id(0) == 0)
    def _():
        st[...] = jnp.zeros_like(st)
        buf[0:8, :] = jnp.zeros((8, wide), F32)

    buf[8 : 8 + Q, :] = xp_ref[...]
    for start in range(0, wide, LANES):
        cols = pl.ds(start, LANES)
        pre = w_ref[taps : taps + 1, cols] + jnp.zeros((Q, LANES), F32)
        for k in range(taps):
            pre = pre + w_ref[k : k + 1, cols] * buf[9 - taps + k : 9 - taps + k + Q, cols]
        pre_ref[:, cols] = pre
        act[:, cols] = (pre * jax.nn.sigmoid(pre)).astype(BF16)
    buf[0:8, :] = buf[Q : Q + 8, :]

    inject = act[:, channels : channels + state_size]
    readout = act[:, channels + state_size :]
    affinity = dot(readout, inject, NT)
    mask = lax.broadcasted_iota(jnp.int32, (Q, Q), 0) >= lax.broadcasted_iota(jnp.int32, (Q, Q), 1)
    first = lax.broadcasted_iota(jnp.int32, (1, LANES), 1) < LANES // 2
    states_ref[0] = st[...].astype(BF16)
    for pair in range(heads // 2):
        cols = pl.ds(pair * LANES, LANES)
        signal = act[:, cols]
        parts = []
        for side in range(2):
            h = 2 * pair + side
            gap = col_ref[:, h : h + 1] - row_ref[h : h + 1, :]
            weights = jnp.where(mask, jnp.exp(gap), 0.0)
            mixing = (affinity * weights * row_ref[DT_AT + h : DT_AT + h + 1, :]).astype(BF16)
            parts.append(dot(mixing, signal))
        within = jnp.where(first, parts[0], parts[1])
        run = jnp.where(first, col_ref[:, 2 * pair : 2 * pair + 1], col_ref[:, 2 * pair + 1 : 2 * pair + 2])
        step = jnp.where(
            first,
            col_ref[:, DT_AT + 2 * pair : DT_AT + 2 * pair + 1],
            col_ref[:, DT_AT + 2 * pair + 1 : DT_AT + 2 * pair + 2],
        )
        end = run[Q - 1 : Q, :]
        before = st[:, cols]
        across = jnp.exp(run) * dot(readout, before.astype(BF16))
        wide_signal = signal.astype(F32)
        mixed_ref[:, cols] = within + across + skip_ref[:, cols] * wide_signal
        weighted = (jnp.exp(end - run) * step * wide_signal).astype(BF16)
        st[:, cols] = jnp.exp(end) * before + dot(inject, weighted, TN)


def scan_backward(
    heads, taps, passed, xp_ref, pre_ref, col_ref, row_ref, w_ref, skip_ref, states_ref, dy_ref,
    gw_in, dst_in, carry_in, *refs,
):
    dx_ref, dbc_ref, colout_ref, rowout_ref, sums_ref, gw_ref, dst_out, carry_out, buf, dst, dgs = refs[passed:]
    channels = skip_ref.shape[1]
    wide = xp_ref.shape[1]
    state_size = (wide - channels) // 2

    @pl.when(pl.program_id(0) == 0)
    def _():
        dst[...] = dst_in[...]
        buf[Q : Q + 8, :] = carry_in[...]
        gw_ref[...] = gw_in[...]

    def act_of(start):
        pre = pre_ref[:, pl.ds(start, LANES)]
        return (pre * jax.nn.sigmoid(pre)).astype(BF16)

    def conv_back(start, d_act):
        cols = pl.ds(start, LANES)
        pre = pre_ref[:, cols]
        s = jax.nn.sigmoid(pre)
        d_pre = d_act * s * (1.0 + pre * (1.0 - s))
        buf[0:Q, cols] = d_pre
        own = xp_ref[:, cols]
        total = jnp.zeros((Q, LANES), F32)
        for k in range(taps):
            moved = buf[taps - 1 - k : taps - 1 - k + Q, cols]
            total = total + w_ref[k : k + 1, cols] * moved
            gw_ref[k : k + 1, cols] += jnp.sum(own * moved, axis=0, keepdims=True)
        gw_ref[taps : taps + 1, cols] += jnp.sum(d_pre, axis=0, keepdims=True)
        buf[Q : Q + 8, cols] = d_pre[0:8, :]
        return total.astype(BF16)

    inject = act_of(channels)
    readout = act_of(channels + state_size)
    affinity = dot(readout, inject, NT)
    mask = lax.broadcasted_iota(jnp.int32, (Q, Q), 0) >= lax.broadcasted_iota(jnp.int32, (Q, Q), 1)
    lane = lax.broadcasted_iota(jnp.int32, (1, LANES), 1)
    first = lane < LANES // 2
    d_inject = jnp.zeros((Q, state_size), F32)
    d_readout = jnp.zeros((Q, state_size), F32)
    colout = jnp.zeros((Q, LANES), F32)
    dgs[...] = jnp.zeros_like(dgs)
    for pair in range(heads // 2):
        cols = pl.ds(pair * LANES, LANES)
        signal = act_of(pair * LANES)
        wide_signal = signal.astype(F32)
        d_low = dy_ref[:, cols]
        d_wide = d_low.astype(F32)
        before = states_ref[0, :, cols]
        d_after = dst[:, cols]
        d_after_low = d_after.astype(BF16)
        run = jnp.where(first, col_ref[:, 2 * pair : 2 * pair + 1], col_ref[:, 2 * pair + 1 : 2 * pair + 2])
        step = jnp.where(
            first,
            col_ref[:, DT_AT + 2 * pair : DT_AT + 2 * pair + 1],
            col_ref[:, DT_AT + 2 * pair + 1 : DT_AT + 2 * pair + 2],
        )
        end = run[Q - 1 : Q, :]
        grown = jnp.exp(run)
        to_end = jnp.exp(end - run)
        d_across = (grown * d_wide).astype(BF16)
        across_part = grown * d_wide * dot(readout, before)
        from_state = dot(inject, d_after_low)
        end_part = wide_signal * from_state
        d_readout += dot(d_across, before, NT)
        d_inject += dot((to_end * step * wide_signal).astype(BF16), d_after_low, NT)
        parts = []
        for side in range(2):
            h = 2 * pair + side
            mine = first if side == 0 else ~first
            gap = col_ref[:, h : h + 1] - row_ref[h : h + 1, :]
            weights = jnp.where(mask, jnp.exp(gap), 0.0)
            stepped = weights * row_ref[DT_AT + h : DT_AT + h + 1, :]
            plain = affinity * weights
            d_mixing = dot(d_low, jnp.where(mine, signal, jnp.zeros_like(signal)), NT)
            dgs[...] += d_mixing * stepped
            pulled = d_mixing * plain
            rowout_ref[h : h + 1, :] = jnp.sum(pulled, axis=0, keepdims=True)
            along = jnp.sum(pulled * row_ref[DT_AT + h : DT_AT + h + 1, :], axis=1, keepdims=True)
            along = along + jnp.sum(jnp.where(mine, across_part, 0.0), axis=1, keepdims=True)
            ended = jnp.sum(jnp.where(mine, end_part, 0.0), axis=1, keepdims=True)
            colout = jnp.where(lane == h, along, colout)
            colout = jnp.where(lane == DT_AT + h, ended, colout)
            parts.append(dot(plain.astype(BF16), d_low, TN))
        within = jnp.where(first, parts[0], parts[1])
        d_signal = step * (within + to_end * from_state) + skip_ref[:, cols] * d_wide
        grown_end = jnp.exp(end)
        sums_ref[0, 0:1, cols] = grown_end * jnp.sum(d_after * before.astype(F32), axis=0, keepdims=True)
        sums_ref[0, 1:2, cols] = jnp.sum(d_wide * wide_signal, axis=0, keepdims=True)
        dst[:, cols] = grown_end * d_after + dot(readout, d_across, TN)
        dx_ref[:, cols] = conv_back(pair * LANES, d_signal)
    colout_ref[...] = colout
    d_affinity = dgs[...].astype(BF16)
    d_readout += dot(d_affinity, inject)
    d_inject += dot(d_affinity, readout, TN)
    dbc_ref[:, :state_size] = conv_back(channels, d_inject)
    dbc_ref[:, state_size:] = conv_back(channels + state_size, d_readout)

    @pl.when(pl.program_id(0) == pl.num_programs(0) - 1)
    def _():
        dst_out[...] = dst[...]
        carry_out[...] = buf[Q : Q + 8, :]


def whole_block(shape):
    return pl.BlockSpec(shape, lambda i: (0,) * len(shape))


def run_forward(xp, col, row, w, skip, heads, taps, after):
    length, wide = xp.shape[0], w.shape[1]
    channels = skip.shape[1]
    chunks = length // Q
    state_size = (wide - channels) // 2
    return pl.pallas_call(
        functools.partial(scan_forward, heads, taps),
        grid=(chunks,),
        in_specs=[
            pl.BlockSpec((Q, wide), lambda i: (i, 0)),
            pl.BlockSpec((Q, LANES), lambda i: (i, 0)),
            pl.BlockSpec((2 * DT_AT, Q), lambda i: (0, i)),
            whole_block(w.shape),
            whole_block(skip.shape),
            pl.BlockSpec(memory_space=pl.ANY),
        ],
        out_specs=[
            pl.BlockSpec((Q, channels), lambda i: (i, 0)),
            pl.BlockSpec((Q, wide), lambda i: (i, 0)),
            pl.BlockSpec((1, state_size, channels), lambda i: (i, 0, 0)),
        ],
        out_shape=[
            jax.ShapeDtypeStruct((length, channels), F32),
            jax.ShapeDtypeStruct((length, wide), F32),
            jax.ShapeDtypeStruct((chunks, state_size, channels), BF16),
        ],
        scratch_shapes=[
            pltpu.VMEM((Q + 8, wide), F32),
            pltpu.VMEM((Q, wide), BF16),
            pltpu.VMEM((state_size, channels), F32),
        ],
        compiler_params=pltpu.CompilerParams(vmem_limit_bytes=40 * 2**20),
        cost_estimate=pl.CostEstimate(flops=20 * 10**9, bytes_accessed=13 * 10**6, transcendentals=5 * 10**6),
        name="scan_forward",
    )(xp, col, row, w, skip, after)


def run_backward(low, high, kept, after, xp, pre, col, row, w, skip, states, dy, heads, taps):
    length, wide = pre.shape
    channels = skip.shape[1]
    chunks = length // Q
    state_size = (wide - channels) // 2
    back = lambda i: (high - 1 - i, 0)
    across = lambda i: (0, high - 1 - i)
    first = lambda i: (high - 1 - i, 0, 0)
    if kept is None:
        buffers = []
        carries = [jnp.zeros(w.shape, F32), jnp.zeros((state_size, channels), F32), jnp.zeros((8, wide), F32)]
    else:
        buffers, carries = list(kept[:5]), list(kept[5:])
    anywhere = pl.BlockSpec(memory_space=pl.ANY)
    passed = len(buffers) + len(after)
    return pl.pallas_call(
        functools.partial(scan_backward, heads, taps, passed),
        grid=(high - low,),
        in_specs=[
            pl.BlockSpec((Q, wide), back),
            pl.BlockSpec((Q, wide), back),
            pl.BlockSpec((Q, LANES), back),
            pl.BlockSpec((2 * DT_AT, Q), across),
            whole_block(w.shape),
            whole_block(skip.shape),
            pl.BlockSpec((1, state_size, channels), first),
            pl.BlockSpec((Q, channels), back),
            whole_block(w.shape),
            whole_block((state_size, channels)),
            whole_block((8, wide)),
        ]
        + [anywhere] * passed,
        out_specs=[
            pl.BlockSpec((Q, channels), back),
            pl.BlockSpec((Q, 2 * state_size), back),
            pl.BlockSpec((Q, LANES), back),
            pl.BlockSpec((DT_AT, Q), across),
            pl.BlockSpec((1, 2, channels), first),
            whole_block(w.shape),
            whole_block((state_size, channels)),
            whole_block((8, wide)),
        ],
        out_shape=[
            jax.ShapeDtypeStruct((length, channels), BF16),
            jax.ShapeDtypeStruct((length, 2 * state_size), BF16),
            jax.ShapeDtypeStruct((length, LANES), F32),
            jax.ShapeDtypeStruct((DT_AT, length), F32),
            jax.ShapeDtypeStruct((chunks, 2, channels), F32),
            jax.ShapeDtypeStruct(w.shape, F32),
            jax.ShapeDtypeStruct((state_size, channels), F32),
            jax.ShapeDtypeStruct((8, wide), F32),
        ],
        scratch_shapes=[
            pltpu.VMEM((Q + 8, wide), F32),
            pltpu.VMEM((state_size, channels), F32),
            pltpu.VMEM((Q, Q), F32),
        ],
        input_output_aliases={11 + k: k for k in range(len(buffers))},
        compiler_params=pltpu.CompilerParams(vmem_limit_bytes=40 * 2**20),
        cost_estimate=pl.CostEstimate(
            flops=(high - low) * 8 * 10**9, bytes_accessed=(high - low) * 4 * 10**6, transcendentals=10**6
        ),
        name="scan_backward",
    )(xp, pre, col, row, w, skip, states, dy, *carries, *buffers, *after)


def swap(x, axis, bit):
    size = lax.axis_size(axis)
    return lax.ppermute(x, axis, [(i, i ^ bit) for i in range(size)])


def bits_of(axis):
    size = lax.axis_size(axis)
    return [1 << k for k in range(size.bit_length() - 1)]


def my_bit(axis, bit):
    return (lax.axis_index(axis) // bit) % 2


def both(own, other, second):
    return jnp.where(second == 1, jnp.stack([other, own]), jnp.stack([own, other]))


def gather_rows(block, order):
    bits = bits_of("dp")
    x = block
    for bit in order:
        last = x
        x = both(x, swap(x, "dp", bit), my_bit("dp", bit))
    done = order[::-1]
    axes = [done.index(b) for b in bits[::-1]]
    count = len(bits)
    x = jnp.transpose(x, axes + list(range(count, count + block.ndim)))
    return x.reshape((-1,) + block.shape[1:]), last


def scatter_rows(parts):
    bits = bits_of("dp")
    left = bits[::-1]
    parts = [x.reshape((2,) * len(bits) + (x.shape[0] >> len(bits), x.shape[1])) for x in parts]
    for bit in bits:
        axis = left.index(bit)
        mine = my_bit("dp", bit)
        keep = [lax.dynamic_index_in_dim(x, mine, axis, keepdims=False) for x in parts]
        send = [lax.dynamic_index_in_dim(x, 1 - mine, axis, keepdims=False).astype(BF16) for x in parts]
        keep, send = (jnp.concatenate(x, axis=-1) if len(x) > 1 else x[0] for x in (keep, send))
        yield send
        parts = [keep + swap(send, "dp", bit).astype(F32)]
        left.remove(bit)
    yield parts[0]


def sum_dp(x):
    for bit in bits_of("dp"):
        x = x + swap(x, "dp", bit)
    return x


def body(
    residual, grad_out, norm_gain, w_zx, w_dt, w_bc, conv_x, conv_x_bias, conv_bc, conv_bc_bias,
    dt_bias, a_log, d_skip, gate_gain, w_out,
):
    own_rows, width = residual.shape
    channels = gate_gain.shape[0]
    all_channels = channels * lax.axis_size("tensor")
    state_size = w_bc.shape[2]
    heads = dt_bias.shape[0]
    head_size = channels // heads
    taps = conv_x.shape[0]
    wide = channels + 2 * state_size
    side = lax.axis_index("tensor")

    def own_half(x):
        return lax.dynamic_slice_in_dim(x, side * own_rows, own_rows, 0)

    def other_half(x):
        return lax.dynamic_slice_in_dim(x, (1 - side) * own_rows, own_rows, 0)

    pad_dt = LANES - heads
    bits = bits_of("dp")
    far = bits[:1:-1]
    weights_in, _ = gather_rows(
        jnp.concatenate([w_zx[1], w_bc[0], w_bc[1], jnp.pad(w_dt, ((0, 0), (0, pad_dt)))], axis=1),
        far + bits[1:2] + bits[:1],
    )
    weights_side, side_last = gather_rows(
        jnp.concatenate([w_zx[0], w_out.T], axis=1), bits[1:2] + far + bits[:1]
    )
    weight_gate, weight_out_t = weights_side[:, :channels], weights_side[:, channels:]

    rows = both(residual, swap(residual, "tensor", 1), side).reshape(2 * own_rows, width).astype(F32)
    cotangent = both(grad_out, swap(grad_out, "tensor", 1), side).reshape(2 * own_rows, width)
    in_scale = lax.rsqrt(jnp.mean(rows * rows, axis=1, keepdims=True) + EPS)
    normed = (rows * in_scale * norm_gain).astype(BF16)

    projected = dot(normed, weights_in)
    dt_in = projected[:, wide : wide + heads] + dt_bias
    timestep = jax.nn.softplus(dt_in)
    rate = -jnp.exp(a_log)
    decays = timestep * rate
    length = decays.shape[0]
    chunks = length // Q
    tri = jnp.tril(jnp.ones((Q, Q), F32))
    running = jnp.einsum("ij,cjh->cih", tri, decays.reshape(chunks, Q, heads), precision=HIGH)
    running_flat = running.reshape(length, heads)
    gap = jnp.zeros((length, DT_AT - heads), F32)
    packed = jnp.concatenate([running_flat, gap, timestep, gap], axis=1)
    col = jnp.pad(packed, ((0, 0), (0, LANES - 2 * DT_AT)))
    row = packed.T
    taps_all = jnp.concatenate([conv_x, conv_bc[0], conv_bc[1]], axis=1)
    bias_all = jnp.concatenate([conv_x_bias, conv_bc_bias[0], conv_bc_bias[1]])
    w = jnp.concatenate([taps_all, bias_all[None], jnp.zeros((8 - taps - 1, wide), F32)], axis=0)
    skip = jnp.repeat(d_skip, head_size)[None]
    mixed, pre, states = run_forward(projected, col, row, w, skip, heads, taps, side_last)

    gate_pre = dot(normed, weight_gate)
    d_gated = dot(cotangent, weight_out_t)
    logistic = jax.nn.sigmoid(gate_pre)
    gate_act = gate_pre * logistic
    gated_in = mixed * gate_act
    scaled_grad = d_gated * gate_gain
    sums = jnp.stack([jnp.sum(gated_in * gated_in, axis=1), jnp.sum(scaled_grad * gated_in, axis=1)])
    sums = sums + swap(sums, "tensor", 1)
    out_scale = lax.rsqrt(sums[0] / all_channels + EPS)[:, None]
    gated = (gated_in * out_scale * gate_gain).astype(BF16)
    d_inner = out_scale * scaled_grad - gated_in * (out_scale**3 * sums[1][:, None] / all_channels)
    d_mixed = (d_inner * gate_act).astype(BF16)
    d_gate = (d_inner * mixed * logistic * (1.0 + gate_pre * (1.0 - logistic))).astype(BF16)
    grad_gate_gain = jnp.sum(d_gated * gated_in * out_scale, axis=0)

    sent = swap(dot(other_half(gated), weight_out_t, NT).astype(BF16), "tensor", 1)
    branch = dot(own_half(gated), weight_out_t, NT) + sent.astype(F32)
    layer_out = (residual.astype(F32) + branch).astype(BF16)

    steps_side = scatter_rows([dot(normed, d_gate, TN), dot(cotangent, gated, TN)])
    ends = [0] + [chunks * k // 4 for k in range(1, 5)]
    kept = None
    for low, high in ((ends[3], ends[4]), (ends[1], ends[3]), (ends[0], ends[1])):
        if high > low:
            kept = run_backward(
                low, high, kept, [next(steps_side)], projected, pre, col, row, w, skip, states, d_mixed, heads, taps
            )
    d_x, d_bc, colout, rowout, chunk_sums, grad_w = kept[:6]
    *_, grad_side = steps_side

    along = colout[:, :heads].reshape(chunks, Q, heads)
    ended = colout[:, DT_AT : DT_AT + heads].reshape(chunks, Q, heads)
    pulled = rowout[:heads].T.reshape(chunks, Q, heads)
    steps = timestep.reshape(chunks, Q, heads)
    d_step = pulled + jnp.exp(running[:, -1:] - running) * ended
    to_end = steps * jnp.exp(running[:, -1:] - running) * ended
    d_running = along - steps * d_step
    per_head = jnp.sum(chunk_sums.reshape(chunks, 2, heads, head_size), axis=3)
    at_end = jnp.sum(to_end, axis=1) + per_head[:, 0]
    d_decays = jnp.einsum("ji,cjh->cih", tri, d_running, precision=HIGH) + at_end[:, None]
    d_decays = d_decays.reshape(length, heads)
    d_dt = (d_step.reshape(length, heads) + d_decays * rate) * jax.nn.sigmoid(dt_in)
    grad_dt_bias = jnp.sum(d_dt, axis=0)
    grad_a_log = jnp.sum(d_decays * decays, axis=0)
    grad_d_skip = jnp.sum(per_head[:, 1], axis=0)

    d_shared = d_bc.astype(F32) + swap(d_bc, "tensor", 1).astype(F32)
    d_shared = d_shared.astype(BF16)
    d_dt_low = jnp.pad(d_dt.astype(BF16), ((0, 0), (0, pad_dt)))
    d_rest = jnp.concatenate([d_shared, d_dt_low], axis=1)
    d_rest_half = jnp.concatenate([d_shared * 0.5, d_dt_low], axis=1)
    *_, grad_in = scatter_rows([dot(normed, d_x, TN), dot(normed, d_rest, TN)])
    partial = (
        dot(d_gate, weight_gate, NT)
        + dot(d_x, weights_in[:, :channels], NT)
        + dot(d_rest_half, weights_in[:, channels:], NT)
    )
    received = swap(other_half(partial).astype(BF16), "tensor", 1)
    grad_norm_gain = jnp.sum(partial * rows * in_scale, axis=0)

    shared = jnp.concatenate([grad_norm_gain, grad_w[: taps + 1, channels:].reshape(-1)])
    shared = shared + swap(shared, "tensor", 1)
    heads_part = jnp.concatenate([grad_dt_bias, grad_a_log, grad_d_skip])
    small = jnp.concatenate(
        [grad_gate_gain, grad_w[: taps + 1, :channels].reshape(-1), shared, heads_part]
    )
    count = small.shape[0]
    small = jnp.pad(small, (0, -count % 1024)).reshape(-1, LANES)
    small = sum_dp(small).reshape(-1)
    pieces, at = [], 0
    for size in (channels, (taps + 1) * channels, width, (taps + 1) * 2 * state_size, heads, heads, heads):
        pieces.append(small[at : at + size])
        at += size
    sum_gate_gain, sum_conv, sum_norm, sum_bc, sum_dt_bias, sum_a_log, sum_skip = pieces
    sum_conv = sum_conv.reshape(taps + 1, channels)
    sum_bc = sum_bc.reshape(taps + 1, 2, state_size).transpose(1, 0, 2)

    d_normed = own_half(partial) + received.astype(F32)
    own_scale = own_half(in_scale)
    own = residual.astype(F32)
    weighted = d_normed * norm_gain
    d_residual = (
        grad_out.astype(F32)
        + own_scale * weighted
        - own * own_scale**3 * jnp.mean(weighted * own, axis=1, keepdims=True)
    ).astype(BF16)
    return (
        layer_out,
        d_residual,
        sum_norm,
        jnp.stack([grad_side[:, :channels], grad_in[:, :channels]]),
        grad_in[:, wide : wide + heads],
        jnp.stack([grad_in[:, channels : channels + state_size], grad_in[:, channels + state_size : wide]]),
        sum_conv[:taps],
        sum_conv[taps],
        sum_bc[:, :taps],
        sum_bc[:, taps],
        sum_dt_bias,
        sum_a_log,
        sum_skip,
        sum_gate_gain,
        grad_side[:, channels:].T,
    )


def solution(mesh):
    in_specs = (
        P(("dp", "tensor"), None),
        P(("dp", "tensor"), None),
        P(),
        P(None, "dp", "tensor"),
        P("dp", "tensor"),
        P(None, "dp", None),
        P(None, "tensor"),
        P("tensor"),
        P(),
        P(),
        P("tensor"),
        P("tensor"),
        P("tensor"),
        P("tensor"),
        P("tensor", "dp"),
    )
    out_specs = (
        P(("dp", "tensor"), None),
        P(("dp", "tensor"), None),
        P(),
        P(None, "dp", "tensor"),
        P("dp", "tensor"),
        P(None, "dp", None),
        P(None, "tensor"),
        P("tensor"),
        P(),
        P(),
        P("tensor"),
        P("tensor"),
        P("tensor"),
        P("tensor"),
        P("tensor", "dp"),
    )
    return jax.shard_map(body, mesh=mesh, in_specs=in_specs, out_specs=out_specs, check_vma=False)
```

```python
import functools

import jax
import jax.numpy as jnp
from jax import lax
from jax.experimental import pallas as pl
from jax.experimental.pallas import tpu as pltpu
from jax.sharding import PartitionSpec as P

Q = 256
EPS = 1e-05
HIGH = lax.Precision.HIGHEST
F32 = jnp.float32
BF16 = jnp.bfloat16
NN = (((1,), (0,)), ((), ()))
NT = (((1,), (1,)), ((), ()))
TN = (((0,), (0,)), ((), ()))
LANES = 128
DT_AT = 16


def dot(a, b, dims=NN):
    return lax.dot_general(a, b, dims, preferred_element_type=F32)


def rows_of(ref, first, count, columns):
    return ref[pl.ds(first, count), columns]


def scan_forward(heads, taps, xp_ref, col_ref, row_ref, w_ref, skip_ref, _, mixed_ref, pre_ref, states_ref, buf, act, st):
    channels = skip_ref.shape[1]
    wide = xp_ref.shape[1]
    state_size = (wide - channels) // 2

    @pl.when(pl.program_id(0) == 0)
    def _():
        st[...] = jnp.zeros_like(st)
        buf[0:8, :] = jnp.zeros((8, wide), F32)

    buf[8 : 8 + Q, :] = xp_ref[...]
    for start in range(0, wide, LANES):
        cols = pl.ds(start, LANES)
        pre = w_ref[taps : taps + 1, cols] + jnp.zeros((Q, LANES), F32)
        for k in range(taps):
            pre = pre + w_ref[k : k + 1, cols] * buf[9 - taps + k : 9 - taps + k + Q, cols]
        pre_ref[:, cols] = pre
        act[:, cols] = (pre * jax.nn.sigmoid(pre)).astype(BF16)
    buf[0:8, :] = buf[Q : Q + 8, :]

    inject = act[:, channels : channels + state_size]
    readout = act[:, channels + state_size :]
    affinity = dot(readout, inject, NT)
    mask = lax.broadcasted_iota(jnp.int32, (Q, Q), 0) >= lax.broadcasted_iota(jnp.int32, (Q, Q), 1)
    first = lax.broadcasted_iota(jnp.int32, (1, LANES), 1) < LANES // 2
    states_ref[0] = st[...].astype(BF16)
    for pair in range(heads // 2):
        cols = pl.ds(pair * LANES, LANES)
        signal = act[:, cols]
        parts = []
        for side in range(2):
            h = 2 * pair + side
            gap = col_ref[:, h : h + 1] - row_ref[h : h + 1, :]
            weights = jnp.where(mask, jnp.exp(gap), 0.0)
            mixing = (affinity * weights * row_ref[DT_AT + h : DT_AT + h + 1, :]).astype(BF16)
            parts.append(dot(mixing, signal))
        within = jnp.where(first, parts[0], parts[1])
        run = jnp.where(first, col_ref[:, 2 * pair : 2 * pair + 1], col_ref[:, 2 * pair + 1 : 2 * pair + 2])
        step = jnp.where(
            first,
            col_ref[:, DT_AT + 2 * pair : DT_AT + 2 * pair + 1],
            col_ref[:, DT_AT + 2 * pair + 1 : DT_AT + 2 * pair + 2],
        )
        end = run[Q - 1 : Q, :]
        before = st[:, cols]
        across = jnp.exp(run) * dot(readout, before.astype(BF16))
        wide_signal = signal.astype(F32)
        mixed_ref[:, cols] = within + across + skip_ref[:, cols] * wide_signal
        weighted = (jnp.exp(end - run) * step * wide_signal).astype(BF16)
        st[:, cols] = jnp.exp(end) * before + dot(inject, weighted, TN)


def scan_backward(
    heads, taps, passed, xp_ref, pre_ref, col_ref, row_ref, w_ref, skip_ref, states_ref, dy_ref,
    gw_in, dst_in, carry_in, *refs,
):
    dx_ref, dbc_ref, colout_ref, rowout_ref, sums_ref, gw_ref, dst_out, carry_out, buf, dst, dgs = refs[passed:]
    channels = skip_ref.shape[1]
    wide = xp_ref.shape[1]
    state_size = (wide - channels) // 2

    @pl.when(pl.program_id(0) == 0)
    def _():
        dst[...] = dst_in[...]
        buf[Q : Q + 8, :] = carry_in[...]
        gw_ref[...] = gw_in[...]

    def act_of(start):
        pre = pre_ref[:, pl.ds(start, LANES)]
        return (pre * jax.nn.sigmoid(pre)).astype(BF16)

    def conv_back(start, d_act):
        cols = pl.ds(start, LANES)
        pre = pre_ref[:, cols]
        s = jax.nn.sigmoid(pre)
        d_pre = d_act * s * (1.0 + pre * (1.0 - s))
        buf[0:Q, cols] = d_pre
        own = xp_ref[:, cols]
        total = jnp.zeros((Q, LANES), F32)
        for k in range(taps):
            moved = buf[taps - 1 - k : taps - 1 - k + Q, cols]
            total = total + w_ref[k : k + 1, cols] * moved
            gw_ref[k : k + 1, cols] += jnp.sum(own * moved, axis=0, keepdims=True)
        gw_ref[taps : taps + 1, cols] += jnp.sum(d_pre, axis=0, keepdims=True)
        buf[Q : Q + 8, cols] = d_pre[0:8, :]
        return total.astype(BF16)

    inject = act_of(channels)
    readout = act_of(channels + state_size)
    affinity = dot(readout, inject, NT)
    mask = lax.broadcasted_iota(jnp.int32, (Q, Q), 0) >= lax.broadcasted_iota(jnp.int32, (Q, Q), 1)
    lane = lax.broadcasted_iota(jnp.int32, (1, LANES), 1)
    first = lane < LANES // 2
    d_inject = jnp.zeros((Q, state_size), F32)
    d_readout = jnp.zeros((Q, state_size), F32)
    colout = jnp.zeros((Q, LANES), F32)
    dgs[...] = jnp.zeros_like(dgs)
    for pair in range(heads // 2):
        cols = pl.ds(pair * LANES, LANES)
        signal = act_of(pair * LANES)
        wide_signal = signal.astype(F32)
        d_low = dy_ref[:, cols]
        d_wide = d_low.astype(F32)
        before = states_ref[0, :, cols]
        d_after = dst[:, cols]
        d_after_low = d_after.astype(BF16)
        run = jnp.where(first, col_ref[:, 2 * pair : 2 * pair + 1], col_ref[:, 2 * pair + 1 : 2 * pair + 2])
        step = jnp.where(
            first,
            col_ref[:, DT_AT + 2 * pair : DT_AT + 2 * pair + 1],
            col_ref[:, DT_AT + 2 * pair + 1 : DT_AT + 2 * pair + 2],
        )
        end = run[Q - 1 : Q, :]
        grown = jnp.exp(run)
        to_end = jnp.exp(end - run)
        d_across = (grown * d_wide).astype(BF16)
        across_part = grown * d_wide * dot(readout, before)
        from_state = dot(inject, d_after_low)
        end_part = wide_signal * from_state
        d_readout += dot(d_across, before, NT)
        d_inject += dot((to_end * step * wide_signal).astype(BF16), d_after_low, NT)
        parts = []
        for side in range(2):
            h = 2 * pair + side
            mine = first if side == 0 else ~first
            gap = col_ref[:, h : h + 1] - row_ref[h : h + 1, :]
            weights = jnp.where(mask, jnp.exp(gap), 0.0)
            stepped = weights * row_ref[DT_AT + h : DT_AT + h + 1, :]
            plain = affinity * weights
            d_mixing = dot(d_low, jnp.where(mine, signal, jnp.zeros_like(signal)), NT)
            dgs[...] += d_mixing * stepped
            pulled = d_mixing * plain
            rowout_ref[h : h + 1, :] = jnp.sum(pulled, axis=0, keepdims=True)
            along = jnp.sum(pulled * row_ref[DT_AT + h : DT_AT + h + 1, :], axis=1, keepdims=True)
            along = along + jnp.sum(jnp.where(mine, across_part, 0.0), axis=1, keepdims=True)
            ended = jnp.sum(jnp.where(mine, end_part, 0.0), axis=1, keepdims=True)
            colout = jnp.where(lane == h, along, colout)
            colout = jnp.where(lane == DT_AT + h, ended, colout)
            parts.append(dot(plain.astype(BF16), d_low, TN))
        within = jnp.where(first, parts[0], parts[1])
        d_signal = step * (within + to_end * from_state) + skip_ref[:, cols] * d_wide
        grown_end = jnp.exp(end)
        sums_ref[0, 0:1, cols] = grown_end * jnp.sum(d_after * before.astype(F32), axis=0, keepdims=True)
        sums_ref[0, 1:2, cols] = jnp.sum(d_wide * wide_signal, axis=0, keepdims=True)
        dst[:, cols] = grown_end * d_after + dot(readout, d_across, TN)
        dx_ref[:, cols] = conv_back(pair * LANES, d_signal)
    colout_ref[...] = colout
    d_affinity = dgs[...].astype(BF16)
    d_readout += dot(d_affinity, inject)
    d_inject += dot(d_affinity, readout, TN)
    dbc_ref[:, :state_size] = conv_back(channels, d_inject)
    dbc_ref[:, state_size:] = conv_back(channels + state_size, d_readout)

    @pl.when(pl.program_id(0) == pl.num_programs(0) - 1)
    def _():
        dst_out[...] = dst[...]
        carry_out[...] = buf[Q : Q + 8, :]


def whole_block(shape):
    return pl.BlockSpec(shape, lambda i: (0,) * len(shape))


def run_forward(xp, col, row, w, skip, heads, taps, after):
    length, wide = xp.shape[0], w.shape[1]
    channels = skip.shape[1]
    chunks = length // Q
    state_size = (wide - channels) // 2
    return pl.pallas_call(
        functools.partial(scan_forward, heads, taps),
        grid=(chunks,),
        in_specs=[
            pl.BlockSpec((Q, wide), lambda i: (i, 0)),
            pl.BlockSpec((Q, LANES), lambda i: (i, 0)),
            pl.BlockSpec((2 * DT_AT, Q), lambda i: (0, i)),
            whole_block(w.shape),
            whole_block(skip.shape),
            pl.BlockSpec(memory_space=pl.ANY),
        ],
        out_specs=[
            pl.BlockSpec((Q, channels), lambda i: (i, 0)),
            pl.BlockSpec((Q, wide), lambda i: (i, 0)),
            pl.BlockSpec((1, state_size, channels), lambda i: (i, 0, 0)),
        ],
        out_shape=[
            jax.ShapeDtypeStruct((length, channels), F32),
            jax.ShapeDtypeStruct((length, wide), F32),
            jax.ShapeDtypeStruct((chunks, state_size, channels), BF16),
        ],
        scratch_shapes=[
            pltpu.VMEM((Q + 8, wide), F32),
            pltpu.VMEM((Q, wide), BF16),
            pltpu.VMEM((state_size, channels), F32),
        ],
        compiler_params=pltpu.CompilerParams(vmem_limit_bytes=40 * 2**20),
        cost_estimate=pl.CostEstimate(flops=20 * 10**9, bytes_accessed=13 * 10**6, transcendentals=5 * 10**6),
        name="scan_forward",
    )(xp, col, row, w, skip, after)


def run_backward(low, high, kept, after, xp, pre, col, row, w, skip, states, dy, heads, taps):
    length, wide = pre.shape
    channels = skip.shape[1]
    chunks = length // Q
    state_size = (wide - channels) // 2
    back = lambda i: (high - 1 - i, 0)
    across = lambda i: (0, high - 1 - i)
    first = lambda i: (high - 1 - i, 0, 0)
    if kept is None:
        buffers = []
        carries = [jnp.zeros(w.shape, F32), jnp.zeros((state_size, channels), F32), jnp.zeros((8, wide), F32)]
    else:
        buffers, carries = list(kept[:5]), list(kept[5:])
    anywhere = pl.BlockSpec(memory_space=pl.ANY)
    passed = len(buffers) + len(after)
    return pl.pallas_call(
        functools.partial(scan_backward, heads, taps, passed),
        grid=(high - low,),
        in_specs=[
            pl.BlockSpec((Q, wide), back),
            pl.BlockSpec((Q, wide), back),
            pl.BlockSpec((Q, LANES), back),
            pl.BlockSpec((2 * DT_AT, Q), across),
            whole_block(w.shape),
            whole_block(skip.shape),
            pl.BlockSpec((1, state_size, channels), first),
            pl.BlockSpec((Q, channels), back),
            whole_block(w.shape),
            whole_block((state_size, channels)),
            whole_block((8, wide)),
        ]
        + [anywhere] * passed,
        out_specs=[
            pl.BlockSpec((Q, channels), back),
            pl.BlockSpec((Q, 2 * state_size), back),
            pl.BlockSpec((Q, LANES), back),
            pl.BlockSpec((DT_AT, Q), across),
            pl.BlockSpec((1, 2, channels), first),
            whole_block(w.shape),
            whole_block((state_size, channels)),
            whole_block((8, wide)),
        ],
        out_shape=[
            jax.ShapeDtypeStruct((length, channels), BF16),
            jax.ShapeDtypeStruct((length, 2 * state_size), BF16),
            jax.ShapeDtypeStruct((length, LANES), F32),
            jax.ShapeDtypeStruct((DT_AT, length), F32),
            jax.ShapeDtypeStruct((chunks, 2, channels), F32),
            jax.ShapeDtypeStruct(w.shape, F32),
            jax.ShapeDtypeStruct((state_size, channels), F32),
            jax.ShapeDtypeStruct((8, wide), F32),
        ],
        scratch_shapes=[
            pltpu.VMEM((Q + 8, wide), F32),
            pltpu.VMEM((state_size, channels), F32),
            pltpu.VMEM((Q, Q), F32),
        ],
        input_output_aliases={11 + k: k for k in range(len(buffers))},
        compiler_params=pltpu.CompilerParams(vmem_limit_bytes=40 * 2**20),
        cost_estimate=pl.CostEstimate(
            flops=(high - low) * 8 * 10**9, bytes_accessed=(high - low) * 4 * 10**6, transcendentals=10**6
        ),
        name="scan_backward",
    )(xp, pre, col, row, w, skip, states, dy, *carries, *buffers, *after)


def nothing(*refs):
    pass


def hold(x, after):
    anywhere = pl.BlockSpec(memory_space=pl.ANY)
    return pl.pallas_call(
        nothing,
        in_specs=[anywhere] * 2,
        out_specs=anywhere,
        out_shape=jax.ShapeDtypeStruct(x.shape, x.dtype),
        input_output_aliases={0: 0},
        name="hold",
    )(x, after)


def swap(x, axis, bit):
    size = lax.axis_size(axis)
    return lax.ppermute(x, axis, [(i, i ^ bit) for i in range(size)])


def bits_of(axis):
    size = lax.axis_size(axis)
    return [1 << k for k in range(size.bit_length() - 1)]


def my_bit(axis, bit):
    return (lax.axis_index(axis) // bit) % 2


def both(own, other, second):
    return jnp.where(second == 1, jnp.stack([other, own]), jnp.stack([own, other]))


def gather_rows(block, order):
    bits = bits_of("dp")
    x = block
    for bit in order:
        last = x
        x = both(x, swap(x, "dp", bit), my_bit("dp", bit))
    done = order[::-1]
    axes = [done.index(b) for b in bits[::-1]]
    count = len(bits)
    x = jnp.transpose(x, axes + list(range(count, count + block.ndim)))
    return x.reshape((-1,) + block.shape[1:]), last


def scatter_rows(parts):
    bits = bits_of("dp")
    left = bits[::-1]
    parts = [x.reshape((2,) * len(bits) + (x.shape[0] >> len(bits), x.shape[1])) for x in parts]
    for bit in bits:
        axis = left.index(bit)
        mine = my_bit("dp", bit)
        keep = [lax.dynamic_index_in_dim(x, mine, axis, keepdims=False) for x in parts]
        send = [lax.dynamic_index_in_dim(x, 1 - mine, axis, keepdims=False).astype(BF16) for x in parts]
        keep, send = (jnp.concatenate(x, axis=-1) if len(x) > 1 else x[0] for x in (keep, send))
        yield send
        parts = [keep + swap(send, "dp", bit).astype(F32)]
        left.remove(bit)
    yield parts[0]


def sum_dp(x):
    for bit in bits_of("dp"):
        x = x + swap(x, "dp", bit)
    return x


def body(
    residual, grad_out, norm_gain, w_zx, w_dt, w_bc, conv_x, conv_x_bias, conv_bc, conv_bc_bias,
    dt_bias, a_log, d_skip, gate_gain, w_out,
):
    own_rows, width = residual.shape
    channels = gate_gain.shape[0]
    all_channels = channels * lax.axis_size("tensor")
    state_size = w_bc.shape[2]
    heads = dt_bias.shape[0]
    head_size = channels // heads
    taps = conv_x.shape[0]
    wide = channels + 2 * state_size
    side = lax.axis_index("tensor")

    def own_half(x):
        return lax.dynamic_slice_in_dim(x, side * own_rows, own_rows, 0)

    def other_half(x):
        return lax.dynamic_slice_in_dim(x, (1 - side) * own_rows, own_rows, 0)

    pad_dt = LANES - heads
    bits = bits_of("dp")
    far = bits[:1:-1]
    weights_in, _ = gather_rows(
        jnp.concatenate([w_zx[1], w_bc[0], w_bc[1], jnp.pad(w_dt, ((0, 0), (0, pad_dt)))], axis=1),
        far + bits[1:2] + bits[:1],
    )
    weights_side, side_last = gather_rows(
        jnp.concatenate([w_zx[0], w_out.T], axis=1), bits[1:2] + far + bits[:1]
    )
    weight_gate, weight_out_t = weights_side[:, :channels], weights_side[:, channels:]

    rows = both(residual, swap(residual, "tensor", 1), side).reshape(2 * own_rows, width).astype(F32)
    in_scale = lax.rsqrt(jnp.mean(rows * rows, axis=1, keepdims=True) + EPS)
    normed = (rows * in_scale * norm_gain).astype(BF16)

    projected = dot(normed, weights_in)
    held_grad = hold(grad_out, projected)
    cotangent = both(held_grad, swap(held_grad, "tensor", 1), side).reshape(2 * own_rows, width)
    dt_in = projected[:, wide : wide + heads] + dt_bias
    timestep = jax.nn.softplus(dt_in)
    rate = -jnp.exp(a_log)
    decays = timestep * rate
    length = decays.shape[0]
    chunks = length // Q
    tri = jnp.tril(jnp.ones((Q, Q), F32))
    running = jnp.einsum("ij,cjh->cih", tri, decays.reshape(chunks, Q, heads), precision=HIGH)
    running_flat = running.reshape(length, heads)
    gap = jnp.zeros((length, DT_AT - heads), F32)
    packed = jnp.concatenate([running_flat, gap, timestep, gap], axis=1)
    col = jnp.pad(packed, ((0, 0), (0, LANES - 2 * DT_AT)))
    row = packed.T
    taps_all = jnp.concatenate([conv_x, conv_bc[0], conv_bc[1]], axis=1)
    bias_all = jnp.concatenate([conv_x_bias, conv_bc_bias[0], conv_bc_bias[1]])
    w = jnp.concatenate([taps_all, bias_all[None], jnp.zeros((8 - taps - 1, wide), F32)], axis=0)
    skip = jnp.repeat(d_skip, head_size)[None]
    mixed, pre, states = run_forward(projected, col, row, w, skip, heads, taps, side_last)

    gate_pre = dot(normed, weight_gate)
    d_gated = dot(cotangent, weight_out_t)
    logistic = jax.nn.sigmoid(gate_pre)
    gate_act = gate_pre * logistic
    gated_in = mixed * gate_act
    scaled_grad = d_gated * gate_gain
    sums = jnp.stack([jnp.sum(gated_in * gated_in, axis=1), jnp.sum(scaled_grad * gated_in, axis=1)])
    sums = sums + swap(sums, "tensor", 1)
    out_scale = lax.rsqrt(sums[0] / all_channels + EPS)[:, None]
    gated = (gated_in * out_scale * gate_gain).astype(BF16)
    d_inner = out_scale * scaled_grad - gated_in * (out_scale**3 * sums[1][:, None] / all_channels)
    d_mixed = (d_inner * gate_act).astype(BF16)
    d_gate = (d_inner * mixed * logistic * (1.0 + gate_pre * (1.0 - logistic))).astype(BF16)
    grad_gate_gain = jnp.sum(d_gated * gated_in * out_scale, axis=0)

    steps_side = scatter_rows([dot(normed, d_gate, TN), dot(cotangent, gated, TN)])
    kept = None
    for low, high in ((chunks // 2, chunks), (0, chunks // 2)):
        if high > low:
            kept = run_backward(
                low, high, kept, [next(steps_side)], projected, pre, col, row, w, skip, states, d_mixed, heads, taps
            )
        if low > 0:
            to_send = hold(dot(other_half(gated), weight_out_t, NT).astype(BF16), kept[6])
    branch = dot(own_half(gated), weight_out_t, NT) + swap(to_send, "tensor", 1).astype(F32)
    layer_out = (residual.astype(F32) + branch).astype(BF16)
    d_x, d_bc, colout, rowout, chunk_sums, grad_w = kept[:6]
    *_, grad_side = steps_side

    along = colout[:, :heads].reshape(chunks, Q, heads)
    ended = colout[:, DT_AT : DT_AT + heads].reshape(chunks, Q, heads)
    pulled = rowout[:heads].T.reshape(chunks, Q, heads)
    steps = timestep.reshape(chunks, Q, heads)
    d_step = pulled + jnp.exp(running[:, -1:] - running) * ended
    to_end = steps * jnp.exp(running[:, -1:] - running) * ended
    d_running = along - steps * d_step
    per_head = jnp.sum(chunk_sums.reshape(chunks, 2, heads, head_size), axis=3)
    at_end = jnp.sum(to_end, axis=1) + per_head[:, 0]
    d_decays = jnp.einsum("ji,cjh->cih", tri, d_running, precision=HIGH) + at_end[:, None]
    d_decays = d_decays.reshape(length, heads)
    d_dt = (d_step.reshape(length, heads) + d_decays * rate) * jax.nn.sigmoid(dt_in)
    grad_dt_bias = jnp.sum(d_dt, axis=0)
    grad_a_log = jnp.sum(d_decays * decays, axis=0)
    grad_d_skip = jnp.sum(per_head[:, 1], axis=0)

    d_shared = d_bc.astype(F32) + swap(d_bc, "tensor", 1).astype(F32)
    d_shared = d_shared.astype(BF16)
    d_dt_low = jnp.pad(d_dt.astype(BF16), ((0, 0), (0, pad_dt)))
    d_rest = jnp.concatenate([d_shared, d_dt_low], axis=1)
    *_, grad_x = scatter_rows([dot(normed, d_x, TN)])
    *_, grad_rest = scatter_rows([dot(normed, d_rest, TN)])
    partial = (
        dot(d_gate, weight_gate, NT)
        + dot(d_x, weights_in[:, :channels], NT)
        + dot(d_dt_low, weights_in[:, wide:], NT)
    )
    shared_part = dot(own_half(d_shared), weights_in[:, channels:wide], NT)
    received = swap(other_half(partial).astype(BF16), "tensor", 1)
    own = residual.astype(F32)
    own_scale = own_half(in_scale)
    grad_norm_gain = jnp.sum(partial * rows * in_scale, axis=0) + jnp.sum(shared_part * own * own_scale, axis=0)

    shared = jnp.concatenate([grad_norm_gain, grad_w[: taps + 1, channels:].reshape(-1)])
    shared = shared + swap(shared, "tensor", 1)
    heads_part = jnp.concatenate([grad_dt_bias, grad_a_log, grad_d_skip])
    small = jnp.concatenate(
        [grad_gate_gain, grad_w[: taps + 1, :channels].reshape(-1), shared, heads_part]
    )
    count = small.shape[0]
    small = jnp.pad(small, (0, -count % 1024)).reshape(-1, LANES)
    small = sum_dp(small).reshape(-1)
    pieces, at = [], 0
    for size in (channels, (taps + 1) * channels, width, (taps + 1) * 2 * state_size, heads, heads, heads):
        pieces.append(small[at : at + size])
        at += size
    sum_gate_gain, sum_conv, sum_norm, sum_bc, sum_dt_bias, sum_a_log, sum_skip = pieces
    sum_conv = sum_conv.reshape(taps + 1, channels)
    sum_bc = sum_bc.reshape(taps + 1, 2, state_size).transpose(1, 0, 2)

    d_normed = own_half(partial) + shared_part + received.astype(F32)
    weighted = d_normed * norm_gain
    d_residual = (
        grad_out.astype(F32)
        + own_scale * weighted
        - own * own_scale**3 * jnp.mean(weighted * own, axis=1, keepdims=True)
    ).astype(BF16)
    return (
        layer_out,
        d_residual,
        sum_norm,
        jnp.stack([grad_side[:, :channels], grad_x]),
        grad_rest[:, 2 * state_size : 2 * state_size + heads],
        jnp.stack([grad_rest[:, :state_size], grad_rest[:, state_size : 2 * state_size]]),
        sum_conv[:taps],
        sum_conv[taps],
        sum_bc[:, :taps],
        sum_bc[:, taps],
        sum_dt_bias,
        sum_a_log,
        sum_skip,
        sum_gate_gain,
        grad_side[:, channels:].T,
    )


def solution(mesh):
    in_specs = (
        P(("dp", "tensor"), None),
        P(("dp", "tensor"), None),
        P(),
        P(None, "dp", "tensor"),
        P("dp", "tensor"),
        P(None, "dp", None),
        P(None, "tensor"),
        P("tensor"),
        P(),
        P(),
        P("tensor"),
        P("tensor"),
        P("tensor"),
        P("tensor"),
        P("tensor", "dp"),
    )
    out_specs = (
        P(("dp", "tensor"), None),
        P(("dp", "tensor"), None),
        P(),
        P(None, "dp", "tensor"),
        P("dp", "tensor"),
        P(None, "dp", None),
        P(None, "tensor"),
        P("tensor"),
        P(),
        P(),
        P("tensor"),
        P("tensor"),
        P("tensor"),
        P("tensor"),
        P("tensor", "dp"),
    )
    return jax.shard_map(body, mesh=mesh, in_specs=in_specs, out_specs=out_specs, check_vma=False)
```
